32 devices in a mesh: sample: 2 (over x), head: 4 (over z), group: 4 (over y, core).
Axes of the slice: x: 2, y: 2, z: 4, core: 2. Of those that a mesh axis runs over, the one named last changes fastest.
Arguments:
- queries: bfloat16 [4, 4, 128, 8192], P('group', 'sample', None, 'head'), may hold values from -6 to 6
- kv_comp: bfloat16 [2, 4, 4, 128, 1024], P(None, 'group', 'sample', None, 'head'), may hold values from -6 to 6
- kv_prefix: bfloat16 [2, 4, 512, 1024], P(None, 'group', ('sample', 'head')), may hold values from -6 to 6
- grad_out: bfloat16 [4, 4, 128, 8192], P('group', 'sample', None, 'head'), may hold values from -6 to 6
- prompt_len: int32 [4], P('group'), may hold values from 128 to 512, as said below
- comp_len: int32 [4, 4], P('group', 'sample'), may hold values from 32 to 128, as said below
Outputs:
- attended: bfloat16 [4, 4, 128, 8192], P('group', 'sample', None, 'head')
- grad_queries: bfloat16 [4, 4, 128, 8192], P('group', 'sample', None, 'head')
- grad_comp: bfloat16 [2, 4, 4, 128, 1024], P(None, 'group', 'sample', None, 'head')
- grad_prefix: bfloat16 [2, 4, 512, 1024], P(None, 'group', ('sample', 'head'))
The draws below stay inside these ranges and needn't reach their ends.
Inputs may be any that keep to these rules, and one draw needn't show every extreme that they name: `prompt_len`: one group has exactly 512 prompt tokens and another exactly 128. `comp_len`: in every group one rollout has exactly 128 completion tokens and another exactly 32.
All inputs are finite; a program needn't handle non-finite values.
Results may differ from the reference program's by a relative error of at most 0.014.
Values may be sent and summed in bfloat16 or wider, within the bound.
A program may use at most 128 MiB of HBM per device.

```python
import jax
import jax.numpy as jnp
from jax import lax

HQ = 64
KVH = 8
DH = 128
C = 128
GROUPS = 4
ROLL = 4
P_MAX = 512


def draw_queries(key, part):
    key = jax.random.fold_in(key, 3)
    full_shape = (GROUPS, ROLL, C, HQ * DH)
    values = jnp.clip(jax.random.normal(key, full_shape, jnp.float32), -6.0, 6.0)
    return values.astype(jnp.bfloat16)


def draw_kv_prefix(key, part):
    key = jax.random.fold_in(key, 7)
    full_shape = (2, GROUPS, P_MAX, KVH * DH)
    values = jnp.clip(jax.random.normal(key, full_shape, jnp.float32), -6.0, 6.0)
    return values.astype(jnp.bfloat16)


def draw_prompt_len(key, part):
    key = jax.random.fold_in(key, 11)
    first_key, second_key = jax.random.split(key)
    lengths = jax.random.randint(first_key, (GROUPS,), P_MAX // 4, P_MAX + 1)
    order = jax.random.permutation(second_key, GROUPS)
    slots = jnp.arange(GROUPS, dtype=jnp.int32)
    lengths = jnp.where(slots == order[0], P_MAX, lengths)
    lengths = jnp.where(slots == order[1], P_MAX // 4, lengths)
    return lengths.astype(jnp.int32)


def draw_comp_len(key, part):
    key = jax.random.fold_in(key, 13)
    first_key, second_key = jax.random.split(key)
    lengths = jax.random.randint(first_key, (GROUPS, ROLL), C // 4, C + 1)
    row_keys = jax.random.split(second_key, GROUPS)
    orders = jax.vmap(lambda row_key: jax.random.permutation(row_key, ROLL))(row_keys)
    slots = jnp.arange(ROLL, dtype=jnp.int32)[None, :]
    lengths = jnp.where(slots == orders[:, 0:1], C, lengths)
    lengths = jnp.where(slots == orders[:, 1:2], C // 4, lengths)
    return lengths.astype(jnp.int32)


def shard_levels(own_key, shape, cuts, least, largest):
    loudness, own = 1.0, jax.random.fold_in(own_key, 6)
    for position, shards_of in cuts:
        steps = jnp.exp(jax.random.uniform(jax.random.fold_in(own, position), (shards_of,), jnp.float32, least / len(cuts), largest / len(cuts)))
        loudness = loudness * jnp.repeat(steps, shape[position] // shards_of).reshape([-1 if axis == position else 1 for axis in range(len(shape))])
    return loudness


def centred(stream_key, shape, spread, limit, pieces=(), held_as=jnp.bfloat16):
    factor_of = shard_levels(stream_key, shape, pieces, -0.22, 0.18) if pieces else 1.0
    drawn = jax.random.normal(stream_key, shape, jnp.float32) * spread * factor_of
    return jnp.minimum(jnp.maximum(drawn, -limit), limit).astype(held_as)


def setup_inputs(seed: int = 0) -> dict:
    key_of = jax.random.split(jax.random.key(seed), 7)
    queries = draw_queries(jax.random.fold_in(key_of[6], 71), 0)
    kv_comp = centred(key_of[1], (2, GROUPS, ROLL, C, KVH * DH), 1.0, 6.0, ((1, 4), (2, 2), (4, 4)))
    kv_prefix = draw_kv_prefix(jax.random.fold_in(key_of[6], 71), 0)
    grad_out = centred(key_of[3], (GROUPS, ROLL, C, HQ * DH), 1.0, 6.0, ((0, 4), (1, 2), (3, 4)))
    prompt_len = draw_prompt_len(jax.random.fold_in(key_of[6], 71), 0)
    comp_len = draw_comp_len(jax.random.fold_in(key_of[6], 71), 0)
    return {"queries": queries, "kv_comp": kv_comp, "kv_prefix": kv_prefix, "grad_out": grad_out, "prompt_len": prompt_len, "comp_len": comp_len}


def attend_block(query_one, keys_comp, values_comp, keys_prefix, values_prefix, grad_one, prompt_count, comp_counts):
    softmax_scale = 1.0 / (DH ** 0.5)
    prefix_rows = keys_prefix.shape[0]
    comp_rows = keys_comp.shape[1]
    query32 = query_one.astype(jnp.float32)
    grad32 = grad_one.astype(jnp.float32)
    scores_prefix = jnp.einsum('rtjd,pd->rjtp', query32, keys_prefix.astype(jnp.float32)) * softmax_scale
    scores_comp = jnp.einsum('rtjd,rud->rjtu', query32, keys_comp.astype(jnp.float32)) * softmax_scale
    prefix_live = jnp.arange(prefix_rows, dtype=jnp.int32) < prompt_count
    positions = jnp.arange(comp_rows, dtype=jnp.int32)
    causal = positions[None, :] <= positions[:, None]
    query_live = (positions[None, :] < comp_counts[:, None]).astype(jnp.float32)[:, None, :, None]
    scores_prefix = jnp.where(prefix_live, scores_prefix, -jnp.inf)
    scores_comp = jnp.where(causal, scores_comp, -jnp.inf)
    row_max = jnp.maximum(jnp.max(scores_prefix, axis=-1), jnp.max(scores_comp, axis=-1))
    exp_total = jnp.sum(jnp.exp(scores_prefix - row_max[..., None]), axis=-1) + jnp.sum(jnp.exp(scores_comp - row_max[..., None]), axis=-1)
    log_total = row_max + jnp.log(exp_total)
    weights_prefix32 = jnp.exp(scores_prefix - log_total[..., None]) * query_live
    weights_comp32 = jnp.exp(scores_comp - log_total[..., None]) * query_live
    weights_prefix = weights_prefix32.astype(jnp.bfloat16).astype(jnp.float32)
    weights_comp = weights_comp32.astype(jnp.bfloat16).astype(jnp.float32)
    attended = (jnp.einsum('rjtp,pd->rtjd', weights_prefix, values_prefix.astype(jnp.float32)) + jnp.einsum('rjtu,rud->rtjd', weights_comp, values_comp.astype(jnp.float32))).astype(jnp.bfloat16)
    row_dot = jnp.sum(grad32 * attended.astype(jnp.float32), axis=-1)
    row_dot = jnp.transpose(row_dot, (0, 2, 1))[..., None]
    slope_prefix = (weights_prefix32 * (jnp.einsum('rtjd,pd->rjtp', grad32, values_prefix.astype(jnp.float32)) - row_dot)).astype(jnp.bfloat16).astype(jnp.float32)
    slope_comp = (weights_comp32 * (jnp.einsum('rtjd,rud->rjtu', grad32, values_comp.astype(jnp.float32)) - row_dot)).astype(jnp.bfloat16).astype(jnp.float32)
    grad_query = (softmax_scale * (jnp.einsum('rjtp,pd->rtjd', slope_prefix, keys_prefix.astype(jnp.float32)) + jnp.einsum('rjtu,rud->rtjd', slope_comp, keys_comp.astype(jnp.float32)))).astype(jnp.bfloat16)
    grad_key_comp = (softmax_scale * jnp.einsum('rjtu,rtjd->rud', slope_comp, query32)).astype(jnp.bfloat16)
    grad_value_comp = jnp.einsum('rjtu,rtjd->rud', weights_comp, grad32).astype(jnp.bfloat16)
    grad_key_prefix = (softmax_scale * jnp.einsum('rjtp,rtjd->pd', slope_prefix, query32)).astype(jnp.bfloat16)
    grad_value_prefix = jnp.einsum('rjtp,rtjd->pd', weights_prefix, grad32).astype(jnp.bfloat16)
    return attended, grad_query, grad_key_comp, grad_value_comp, grad_key_prefix, grad_value_prefix


def reference(queries, kv_comp, kv_prefix, grad_out, prompt_len, comp_len):
    repeats = HQ // KVH
    query_all = queries.reshape(GROUPS, ROLL, C, KVH, repeats, DH)
    grad_all = grad_out.reshape(GROUPS, ROLL, C, KVH, repeats, DH)
    keys_comp = kv_comp[0].reshape(GROUPS, ROLL, C, KVH, DH)
    values_comp = kv_comp[1].reshape(GROUPS, ROLL, C, KVH, DH)
    keys_prefix = kv_prefix[0].reshape(GROUPS, P_MAX, KVH, DH)
    values_prefix = kv_prefix[1].reshape(GROUPS, P_MAX, KVH, DH)

    def per_group(group_index):
        def per_head(head_index):
            return attend_block(query_all[group_index][:, :, head_index], keys_comp[group_index][:, :, head_index], values_comp[group_index][:, :, head_index], keys_prefix[group_index][:, head_index], values_prefix[group_index][:, head_index], grad_all[group_index][:, :, head_index], prompt_len[group_index], comp_len[group_index])
        return lax.map(per_head, jnp.arange(KVH, dtype=jnp.int32))

    results = lax.map(per_group, jnp.arange(GROUPS, dtype=jnp.int32))
    attended = jnp.transpose(results[0], (0, 2, 3, 1, 4, 5)).reshape(GROUPS, ROLL, C, HQ * DH)
    grad_queries = jnp.transpose(results[1], (0, 2, 3, 1, 4, 5)).reshape(GROUPS, ROLL, C, HQ * DH)
    grad_keys = jnp.transpose(results[2], (0, 2, 3, 1, 4)).reshape(GROUPS, ROLL, C, KVH * DH)
    grad_values = jnp.transpose(results[3], (0, 2, 3, 1, 4)).reshape(GROUPS, ROLL, C, KVH * DH)
    prefix_keys = jnp.transpose(results[4], (0, 2, 1, 3)).reshape(GROUPS, P_MAX, KVH * DH)
    prefix_values = jnp.transpose(results[5], (0, 2, 1, 3)).reshape(GROUPS, P_MAX, KVH * DH)
    return attended, grad_queries, jnp.stack([grad_keys, grad_values]), jnp.stack([prefix_keys, prefix_values])
```

```python
import functools

import jax
import jax.numpy as jnp
from jax import lax
from jax.experimental import pallas as pl
from jax.experimental.pallas import tpu as pltpu
from jax.sharding import PartitionSpec as P

DH = 128
NEG = -1e30
MESH = pl.DeviceIdType.MESH
SCALE = 1.0 / DH**0.5
EXP2_SCALE = SCALE * 1.4426950408889634
F32 = jnp.float32
BF16 = jnp.bfloat16
HEADS_TILE = 2


def dot(a, b, dims):
    return lax.dot_general(a, b, (dims, ((), ())), preferred_element_type=F32)


def kernel(
    samples,
    heads,
    plen_ref,
    clen_ref,
    q_ref,
    g_ref,
    kvc_ref,
    kvp_ref,
    att_ref,
    dq_ref,
    gc_ref,
    gp_ref,
    landed,
    keys,
    values,
    keys_t,
    values_t,
    acc_k,
    acc_v,
    outgoing,
    incoming,
    send_a,
    recv_a,
    send_b,
    recv_b,
):
    peers = samples * heads
    kv_local = kvc_ref.shape[4] // DH
    rollouts, comp_rows = q_ref.shape[1], q_ref.shape[2]
    repeats = q_ref.shape[3] // kvc_ref.shape[4]
    block_rows = kvp_ref.shape[2]
    prefix_rows = block_rows * peers
    all_rows = prefix_rows + comp_rows
    tiles = repeats // HEADS_TILE
    tile_rows = HEADS_TILE * comp_rows
    me = lax.axis_index("sample") * heads + lax.axis_index("head")

    def device(block):
        return {"sample": lax.div(block, heads), "head": lax.rem(block, heads)}

    def ahead(j):
        return lax.rem(me + j, peers)

    def behind(j):
        return lax.rem(me + peers - j, peers)

    def rows_of(block):
        return pl.ds(pl.multiple_of(block * block_rows, block_rows), block_rows)

    def gather_copy(kv, j, to, owner):
        head = lax.rem(to, heads)
        lanes = pl.ds(pl.multiple_of((head * kv_local + kv) * DH, DH), DH)
        return pltpu.make_async_remote_copy(
            src_ref=kvp_ref.at[:, 0, :, lanes],
            dst_ref=landed.at[kv, :, rows_of(owner), :],
            send_sem=send_a.at[kv, j],
            recv_sem=recv_a.at[kv, j],
            device_id=device(to),
            device_id_type=MESH,
        )

    def reduce_copy(kv, j, to, owner):
        return pltpu.make_async_remote_copy(
            src_ref=outgoing.at[kv, :, rows_of(to), :],
            dst_ref=incoming.at[kv, owner],
            send_sem=send_b.at[kv, j],
            recv_sem=recv_b.at[kv, j],
            device_id=device(to),
            device_id_type=MESH,
        )

    barrier = pltpu.get_barrier_semaphore()
    for j in range(1, peers):
        pl.semaphore_signal(barrier, inc=1, device_id=device(ahead(j)), device_id_type=MESH)
    pl.semaphore_wait(barrier, peers - 1)
    for kv in range(kv_local):
        for j in range(1, peers):
            gather_copy(kv, j, ahead(j), me).start()

    my_head = lax.rem(me, heads)
    for kv in range(kv_local):
        lanes = pl.ds(pl.multiple_of((my_head * kv_local + kv) * DH, DH), DH)
        landed[kv, :, rows_of(me), :] = kvp_ref[:, 0, :, lanes]

    row_id = lax.broadcasted_iota(jnp.int32, (comp_rows, comp_rows), 0)
    lane_id = lax.broadcasted_iota(jnp.int32, (comp_rows, comp_rows), 1)
    one_hot = jnp.where(row_id == lane_id, 1.0, 0.0).astype(BF16)
    causal = jnp.where(row_id <= lane_id, 0.0, NEG).astype(BF16)
    prefix_id = lax.broadcasted_iota(jnp.int32, (prefix_rows, comp_rows), 0)
    prefix_bias = jnp.where(prefix_id < plen_ref[0], 0.0, NEG).astype(BF16)
    for r in range(rollouts):
        keys[r, pl.ds(0, prefix_rows), pl.ds(DH, comp_rows)] = prefix_bias
        keys[r, pl.ds(prefix_rows, comp_rows), pl.ds(DH, comp_rows)] = causal
    position = lax.rem(
        lax.broadcasted_iota(jnp.int32, (1, tile_rows), 1), jnp.int32(comp_rows)
    )

    for kv in range(kv_local):
        for r in range(rollouts):
            lanes = pl.ds(kv * DH, DH)
            key_one = kvc_ref[0, 0, r, :, lanes]
            value_one = kvc_ref[1, 0, r, :, lanes]
            keys[r, pl.ds(prefix_rows, comp_rows), pl.ds(0, DH)] = key_one
            values[r, pl.ds(prefix_rows, comp_rows), :] = value_one
            keys_t[r, :, pl.ds(prefix_rows, comp_rows)] = key_one.astype(F32).T.astype(BF16)
            values_t[r, :, pl.ds(prefix_rows, comp_rows)] = value_one.astype(F32).T.astype(BF16)
        for j in range(1, peers):
            gather_copy(kv, j, ahead(j), behind(j)).wait_recv()
        key_prefix = landed[kv, 0]
        value_prefix = landed[kv, 1]
        key_prefix_t = key_prefix.astype(F32).T.astype(BF16)
        value_prefix_t = value_prefix.astype(F32).T.astype(BF16)
        for r in range(rollouts):
            keys[r, pl.ds(0, prefix_rows), pl.ds(0, DH)] = key_prefix
            values[r, pl.ds(0, prefix_rows), :] = value_prefix
            keys_t[r, :, pl.ds(0, prefix_rows)] = key_prefix_t
            values_t[r, :, pl.ds(0, prefix_rows)] = value_prefix_t
        acc_k[...] = jnp.zeros_like(acc_k)
        acc_v[...] = jnp.zeros_like(acc_v)

        def tile_step(i, carry, kv=kv):
            r = lax.div(i, tiles)
            first = kv * repeats + lax.rem(i, tiles) * HEADS_TILE
            lane_of = [
                pl.ds(pl.multiple_of((first + n) * DH, DH), DH) for n in range(HEADS_TILE)
            ]
            queries = [q_ref[0, r, :, lane] for lane in lane_of]
            grads = [g_ref[0, r, :, lane] for lane in lane_of]
            query = jnp.concatenate(queries, axis=0)
            grad = jnp.concatenate(grads, axis=0)
            query_bias = jnp.concatenate([query, jnp.concatenate([one_hot] * HEADS_TILE, axis=0)], axis=1)
            scores = dot(keys[r], query_bias, ((1,), (1,)))
            row_max = jnp.max(scores, axis=0, keepdims=True)
            exps = jnp.exp2((scores - row_max) * EXP2_SCALE)
            total = jnp.sum(exps, axis=0, keepdims=True)
            inverse = jnp.where(position < clen_ref[0, r], 1.0 / total, 0.0)
            weights32 = exps * inverse
            weights = weights32.astype(BF16)
            attended_t = dot(values_t[r], weights, ((1,), (0,))).astype(BF16).astype(F32)
            grad_t = grad.astype(F32).T
            delta = jnp.sum(attended_t * grad_t, axis=0, keepdims=True)
            slopes = dot(values[r], grad, ((1,), (1,)))
            ds = (weights32 * (slopes - delta)).astype(BF16)
            grad_query = (dot(keys_t[r], ds, ((1,), (0,))) * SCALE).T.astype(BF16)
            attended = attended_t.T.astype(BF16)
            for n in range(HEADS_TILE):
                rows = slice(n * comp_rows, (n + 1) * comp_rows)
                att_ref[0, r, :, lane_of[n]] = attended[rows]
                dq_ref[0, r, :, lane_of[n]] = grad_query[rows]
            acc_v[r] += dot(weights, grad, ((1,), (0,)))
            acc_k[r] += dot(ds, query, ((1,), (0,)))
            return carry

        lax.fori_loop(0, rollouts * tiles, tile_step, 0)

        for r in range(rollouts):
            comp = pl.ds(prefix_rows, comp_rows)
            gc_ref[0, 0, r, :, pl.ds(kv * DH, DH)] = (acc_k[r, comp, :] * SCALE).astype(BF16)
            gc_ref[1, 0, r, :, pl.ds(kv * DH, DH)] = acc_v[r, comp, :].astype(BF16)
        prefix = pl.ds(0, prefix_rows)
        key_total = acc_k[0, prefix, :]
        value_total = acc_v[0, prefix, :]
        for r in range(1, rollouts):
            key_total += acc_k[r, prefix, :]
            value_total += acc_v[r, prefix, :]
        outgoing[kv, 0] = (key_total * SCALE).astype(BF16)
        outgoing[kv, 1] = value_total.astype(BF16)
        for j in range(1, peers):
            reduce_copy(kv, j, ahead(j), me).start()
        incoming[kv, me] = outgoing[kv, :, rows_of(me), :]

    for kv in range(kv_local):
        for j in range(1, peers):
            reduce_copy(kv, j, ahead(j), behind(j)).wait_recv()
        for h in range(heads):
            for kind in range(2):
                sum32 = incoming[kv, h, kind].astype(F32)
                for s in range(1, samples):
                    sum32 += incoming[kv, s * heads + h, kind].astype(F32)
                gp_ref[kind, 0, :, pl.ds((h * kv_local + kv) * DH, DH)] = sum32.astype(BF16)
    for kv in range(kv_local):
        for j in range(1, peers):
            gather_copy(kv, j, ahead(j), me).wait_send()
            reduce_copy(kv, j, ahead(j), me).wait_send()


def body(queries, kv_comp, kv_prefix, grad_out, prompt_len, comp_len):
    samples = lax.axis_size("sample")
    heads = lax.axis_size("head")
    peers = samples * heads
    kv_local = kv_comp.shape[4] // DH
    rollouts, comp_rows = queries.shape[1], queries.shape[2]
    block_rows = kv_prefix.shape[2]
    prefix_rows = block_rows * peers
    all_rows = prefix_rows + comp_rows
    vmem = pl.BlockSpec(memory_space=pltpu.VMEM)
    smem = pl.BlockSpec(memory_space=pltpu.SMEM)
    return pl.pallas_call(
        functools.partial(kernel, samples, heads),
        out_shape=(
            jax.ShapeDtypeStruct(queries.shape, BF16),
            jax.ShapeDtypeStruct(queries.shape, BF16),
            jax.ShapeDtypeStruct(kv_comp.shape, BF16),
            jax.ShapeDtypeStruct(kv_prefix.shape, BF16),
        ),
        in_specs=[smem, smem, vmem, vmem, vmem, vmem],
        out_specs=(vmem, vmem, vmem, vmem),
        scratch_shapes=[
            pltpu.VMEM((kv_local, 2, prefix_rows, DH), BF16),
            pltpu.VMEM((rollouts, all_rows, DH + comp_rows), BF16),
            pltpu.VMEM((rollouts, all_rows, DH), BF16),
            pltpu.VMEM((rollouts, DH, all_rows), BF16),
            pltpu.VMEM((rollouts, DH, all_rows), BF16),
            pltpu.VMEM((rollouts, all_rows, DH), F32),
            pltpu.VMEM((rollouts, all_rows, DH), F32),
            pltpu.VMEM((kv_local, 2, prefix_rows, DH), BF16),
            pltpu.VMEM((kv_local, peers, 2, block_rows, DH), BF16),
            pltpu.SemaphoreType.DMA((kv_local, peers)),
            pltpu.SemaphoreType.DMA((kv_local, peers)),
            pltpu.SemaphoreType.DMA((kv_local, peers)),
            pltpu.SemaphoreType.DMA((kv_local, peers)),
        ],
        compiler_params=pltpu.CompilerParams(
            collective_id=0, has_side_effects=True, vmem_limit_bytes=56 * 1024 * 1024
        ),
    )(prompt_len, comp_len, queries, grad_out, kv_comp, kv_prefix)


def solution(mesh):
    return jax.shard_map(
        body,
        mesh=mesh,
        in_specs=(
            P("group", "sample", None, "head"),
            P(None, "group", "sample", None, "head"),
            P(None, "group", ("sample", "head"), None),
            P("group", "sample", None, "head"),
            P("group"),
            P("group", "sample"),
        ),
        out_specs=(
            P("group", "sample", None, "head"),
            P("group", "sample", None, "head"),
            P(None, "group", "sample", None, "head"),
            P(None, "group", ("sample", "head"), None),
        ),
        check_vma=False,
    )
```

```python
import functools

import jax
import jax.numpy as jnp
from jax import lax
from jax.experimental import pallas as pl
from jax.experimental.pallas import tpu as pltpu
from jax.sharding import PartitionSpec as P

DH = 128
NEG = -1e30
MESH = pl.DeviceIdType.MESH
SCALE = 1.0 / DH**0.5
EXP2_SCALE = SCALE * 1.4426950408889634
F32 = jnp.float32
BF16 = jnp.bfloat16


def heads_per_tile(prefix_rows):
    return 4 if prefix_rows <= 1024 else 2


def dot(a, b, dims):
    return lax.dot_general(a, b, (dims, ((), ())), preferred_element_type=F32)


def kernel(
    samples,
    heads,
    plen_ref,
    clen_ref,
    q_ref,
    g_ref,
    kvc_ref,
    kvp_ref,
    att_ref,
    dq_ref,
    gc_ref,
    gp_ref,
    landed,
    keys,
    values,
    keys_t,
    values_t,
    acc_k,
    acc_v,
    held,
    held_ds,
    outgoing,
    incoming,
    send_a,
    recv_a,
    send_b,
    recv_b,
):
    peers = samples * heads
    kv_local = kvc_ref.shape[4] // DH
    rollouts, comp_rows = q_ref.shape[1], q_ref.shape[2]
    repeats = q_ref.shape[3] // kvc_ref.shape[4]
    block_rows = kvp_ref.shape[2]
    prefix_rows = block_rows * peers
    all_rows = prefix_rows + comp_rows
    tile_heads = heads_per_tile(prefix_rows)
    tiles = repeats // tile_heads
    tile_rows = tile_heads * comp_rows
    me = lax.axis_index("sample") * heads + lax.axis_index("head")

    def device(block):
        return {"sample": lax.div(block, heads), "head": lax.rem(block, heads)}

    def ahead(j):
        return lax.rem(me + j, peers)

    def behind(j):
        return lax.rem(me + peers - j, peers)

    def rows_of(block):
        return pl.ds(pl.multiple_of(block * block_rows, block_rows), block_rows)

    def lanes_of(block, kv):
        head = lax.rem(block, heads)
        return pl.ds(pl.multiple_of((head * kv_local + kv) * DH, DH), DH)

    def gather_copy(kv, kind, j, to, owner):
        return pltpu.make_async_remote_copy(
            src_ref=kvp_ref.at[kind, 0, :, lanes_of(to, kv)],
            dst_ref=landed.at[kv, kind, rows_of(owner), :],
            send_sem=send_a.at[kv, kind, j],
            recv_sem=recv_a.at[kv, kind, j],
            device_id=device(to),
            device_id_type=MESH,
        )

    def reduce_copy(kv, kind, j, to, owner):
        return pltpu.make_async_remote_copy(
            src_ref=outgoing.at[kv, kind, rows_of(to), :],
            dst_ref=incoming.at[kv, kind, owner],
            send_sem=send_b.at[kv, kind, j],
            recv_sem=recv_b.at[kv, kind, j],
            device_id=device(to),
            device_id_type=MESH,
        )

    def send_prompt(kv, kind):
        for j in range(1, peers):
            gather_copy(kv, kind, j, ahead(j), me).start()

    def prompt_arrived(kv, kind):
        for j in range(1, peers):
            gather_copy(kv, kind, j, ahead(j), behind(j)).wait_recv()

    barrier = pltpu.get_barrier_semaphore()
    for j in range(1, peers):
        pl.semaphore_signal(barrier, inc=1, device_id=device(ahead(j)), device_id_type=MESH)

    row_id = lax.broadcasted_iota(jnp.int32, (comp_rows, comp_rows), 0)
    lane_id = lax.broadcasted_iota(jnp.int32, (comp_rows, comp_rows), 1)
    one_hot = jnp.where(row_id == lane_id, 1.0, 0.0).astype(BF16)
    causal = jnp.where(row_id <= lane_id, 0.0, NEG).astype(BF16)
    prefix_id = lax.broadcasted_iota(jnp.int32, (prefix_rows, comp_rows), 0)
    prefix_bias = jnp.where(prefix_id < plen_ref[0], 0.0, NEG).astype(BF16)
    prefix = pl.ds(0, prefix_rows)
    comp = pl.ds(prefix_rows, comp_rows)
    for r in range(rollouts):
        keys[r, prefix, pl.ds(DH, comp_rows)] = prefix_bias
        keys[r, comp, pl.ds(DH, comp_rows)] = causal
    for kv in range(kv_local):
        landed[kv, :, rows_of(me), :] = kvp_ref[:, 0, :, lanes_of(me, kv)]
    position = lax.rem(
        lax.broadcasted_iota(jnp.int32, (1, tile_rows), 1), jnp.int32(comp_rows)
    )

    pl.semaphore_wait(barrier, peers - 1)
    send_prompt(0, 0)
    send_prompt(0, 1)

    def tile_place(i, kv):
        r = lax.div(i, tiles)
        first = kv * repeats + lax.rem(i, tiles) * tile_heads
        return r, [pl.ds(pl.multiple_of((first + n) * DH, DH), DH) for n in range(tile_heads)]

    def stacked(ref, r, lanes):
        return jnp.concatenate([ref[0, r, :, lane] for lane in lanes], axis=0)

    def each_tile(step):
        lax.fori_loop(0, rollouts * tiles, step, 0)

    def finish(kv, kind, acc, factor):
        mine = pl.ds(kv * DH, DH)
        total = acc[0, prefix, :]
        for r in range(1, rollouts):
            total += acc[r, prefix, :]
        outgoing[kv, kind] = (total * factor).astype(BF16)
        for j in range(1, peers):
            reduce_copy(kv, kind, j, ahead(j), me).start()
        incoming[kv, kind, me] = outgoing[kv, kind, rows_of(me), :]
        for r in range(rollouts):
            gc_ref[kind, 0, r, :, mine] = (acc[r, comp, :] * factor).astype(BF16)

    for kv in range(kv_local):
        mine = pl.ds(kv * DH, DH)
        for r in range(rollouts):
            key_one = kvc_ref[0, 0, r, :, mine]
            value_one = kvc_ref[1, 0, r, :, mine]
            keys[r, comp, pl.ds(0, DH)] = key_one
            values[r, comp, :] = value_one
            keys_t[r, :, comp] = key_one.astype(F32).T.astype(BF16)
            values_t[r, :, comp] = value_one.astype(F32).T.astype(BF16)
        acc_k[...] = jnp.zeros_like(acc_k)
        acc_v[...] = jnp.zeros_like(acc_v)

        prompt_arrived(kv, 0)
        if kv + 1 < kv_local:
            send_prompt(kv + 1, 0)
            send_prompt(kv + 1, 1)
        key_prefix = landed[kv, 0]
        key_prefix_t = key_prefix.astype(F32).T.astype(BF16)
        for r in range(rollouts):
            keys[r, prefix, pl.ds(0, DH)] = key_prefix
            keys_t[r, :, prefix] = key_prefix_t

        def weigh(i, carry, kv=kv):
            r, lanes = tile_place(i, kv)
            query_bias = jnp.concatenate(
                [stacked(q_ref, r, lanes), jnp.concatenate([one_hot] * tile_heads, axis=0)], axis=1
            )
            scores = dot(keys[r], query_bias, ((1,), (1,)))
            row_max = jnp.max(scores, axis=0, keepdims=True)
            exps = jnp.exp2((scores - row_max) * EXP2_SCALE)
            total = jnp.sum(exps, axis=0, keepdims=True)
            inverse = jnp.where(position < clen_ref[0, r], 1.0 / total, 0.0)
            weights32 = exps * inverse
            held[i] = weights32
            acc_v[r] += dot(weights32.astype(BF16), stacked(g_ref, r, lanes), ((1,), (0,)))
            return carry

        each_tile(weigh)
        finish(kv, 1, acc_v, 1.0)

        prompt_arrived(kv, 1)
        value_prefix = landed[kv, 1]
        value_prefix_t = value_prefix.astype(F32).T.astype(BF16)
        for r in range(rollouts):
            values[r, prefix, :] = value_prefix
            values_t[r, :, prefix] = value_prefix_t

        def slope(i, carry, kv=kv):
            r, lanes = tile_place(i, kv)
            grad = stacked(g_ref, r, lanes)
            weights32 = held[i]
            attended_t = dot(values_t[r], weights32.astype(BF16), ((1,), (0,))).astype(BF16).astype(F32)
            delta = jnp.sum(attended_t * grad.astype(F32).T, axis=0, keepdims=True)
            slopes = dot(values[r], grad, ((1,), (1,)))
            ds = (weights32 * (slopes - delta)).astype(BF16)
            held_ds[i] = ds
            attended = attended_t.T.astype(BF16)
            for n in range(tile_heads):
                att_ref[0, r, :, lanes[n]] = attended[n * comp_rows : (n + 1) * comp_rows]
            acc_k[r] += dot(ds, stacked(q_ref, r, lanes), ((1,), (0,)))
            return carry

        each_tile(slope)
        finish(kv, 0, acc_k, SCALE)

        def query_grad(i, carry, kv=kv):
            r, lanes = tile_place(i, kv)
            grad_query = (dot(keys_t[r], held_ds[i], ((1,), (0,))) * SCALE).T.astype(BF16)
            for n in range(tile_heads):
                dq_ref[0, r, :, lanes[n]] = grad_query[n * comp_rows : (n + 1) * comp_rows]
            return carry

        each_tile(query_grad)

    for kv in range(kv_local):
        for kind in (1, 0):
            for j in range(1, peers):
                reduce_copy(kv, kind, j, ahead(j), behind(j)).wait_recv()
            for h in range(heads):
                sum32 = incoming[kv, kind, h].astype(F32)
                for s in range(1, samples):
                    sum32 += incoming[kv, kind, s * heads + h].astype(F32)
                gp_ref[kind, 0, :, pl.ds((h * kv_local + kv) * DH, DH)] = sum32.astype(BF16)
    for kv in range(kv_local):
        for kind in range(2):
            for j in range(1, peers):
                gather_copy(kv, kind, j, ahead(j), me).wait_send()
                reduce_copy(kv, kind, j, ahead(j), me).wait_send()


def write_out(*refs):
    sources, targets, sems = refs[:4], refs[4:8], refs[8]
    copies = [pltpu.make_async_copy(sources[i], targets[i], sems.at[i]) for i in range(4)]
    for copy in copies:
        copy.start()
    for copy in copies:
        copy.wait()


def body(queries, kv_comp, kv_prefix, grad_out, prompt_len, comp_len):
    samples = lax.axis_size("sample")
    heads = lax.axis_size("head")
    peers = samples * heads
    kv_local = kv_comp.shape[4] // DH
    rollouts, comp_rows = queries.shape[1], queries.shape[2]
    block_rows = kv_prefix.shape[2]
    prefix_rows = block_rows * peers
    all_rows = prefix_rows + comp_rows
    tile_heads = heads_per_tile(prefix_rows)
    tile_count = queries.shape[3] // DH // kv_local // tile_heads * rollouts
    vmem = pl.BlockSpec(memory_space=pltpu.VMEM)
    smem = pl.BlockSpec(memory_space=pltpu.SMEM)
    shapes = (queries.shape, queries.shape, kv_comp.shape, kv_prefix.shape)
    results = pl.pallas_call(
        functools.partial(kernel, samples, heads),
        out_shape=tuple(pltpu.VMEM(shape, BF16) for shape in shapes),
        in_specs=[smem, smem, vmem, vmem, vmem, vmem],
        out_specs=(vmem, vmem, vmem, vmem),
        scratch_shapes=[
            pltpu.VMEM((kv_local, 2, prefix_rows, DH), BF16),
            pltpu.VMEM((rollouts, all_rows, DH + comp_rows), BF16),
            pltpu.VMEM((rollouts, all_rows, DH), BF16),
            pltpu.VMEM((rollouts, DH, all_rows), BF16),
            pltpu.VMEM((rollouts, DH, all_rows), BF16),
            pltpu.VMEM((rollouts, all_rows, DH), F32),
            pltpu.VMEM((rollouts, all_rows, DH), F32),
            pltpu.VMEM((tile_count, all_rows, tile_heads * comp_rows), F32),
            pltpu.VMEM((tile_count, all_rows, tile_heads * comp_rows), BF16),
            pltpu.VMEM((kv_local, 2, prefix_rows, DH), BF16),
            pltpu.VMEM((kv_local, 2, peers, block_rows, DH), BF16),
            pltpu.SemaphoreType.DMA((kv_local, 2, peers)),
            pltpu.SemaphoreType.DMA((kv_local, 2, peers)),
            pltpu.SemaphoreType.DMA((kv_local, 2, peers)),
            pltpu.SemaphoreType.DMA((kv_local, 2, peers)),
        ],
        compiler_params=pltpu.CompilerParams(
            collective_id=0, has_side_effects=True, vmem_limit_bytes=60 * 1024 * 1024
        ),
    )(prompt_len, comp_len, queries, grad_out, kv_comp, kv_prefix)
    return pl.pallas_call(
        write_out,
        out_shape=tuple(jax.ShapeDtypeStruct(shape, BF16) for shape in shapes),
        in_specs=[vmem] * 4,
        out_specs=(pl.BlockSpec(memory_space=pl.ANY),) * 4,
        scratch_shapes=[pltpu.SemaphoreType.DMA((4,))],
    )(*results)


def solution(mesh):
    return jax.shard_map(
        body,
        mesh=mesh,
        in_specs=(
            P("group", "sample", None, "head"),
            P(None, "group", "sample", None, "head"),
            P(None, "group", ("sample", "head"), None),
            P("group", "sample", None, "head"),
            P("group"),
            P("group", "sample"),
        ),
        out_specs=(
            P("group", "sample", None, "head"),
            P("group", "sample", None, "head"),
            P(None, "group", "sample", None, "head"),
            P(None, "group", ("sample", "head"), None),
        ),
        check_vma=False,
    )
```

```python
import functools

import jax
import jax.numpy as jnp
from jax import lax
from jax.experimental import pallas as pl
from jax.experimental.pallas import tpu as pltpu
from jax.sharding import PartitionSpec as P

DH = 128
NEG = -1e30
MESH = pl.DeviceIdType.MESH
SCALE = 1.0 / DH**0.5
EXP2_SCALE = SCALE * 1.4426950408889634
F32 = jnp.float32
BF16 = jnp.bfloat16


def heads_per_tile(prefix_rows):
    return 8 if prefix_rows <= 1024 else 2


def dot(a, b, dims):
    return lax.dot_general(a, b, (dims, ((), ())), preferred_element_type=F32)


def kernel(
    samples,
    heads,
    plen_ref,
    clen_ref,
    q_ref,
    g_ref,
    kvc_ref,
    kvp_ref,
    att_ref,
    dq_ref,
    gc_ref,
    gp_ref,
    landed,
    keys,
    values,
    keys_t,
    values_t,
    acc_k,
    acc_v,
    held,
    held_ds,
    outgoing,
    incoming,
    send_a,
    recv_a,
    send_b,
    recv_b,
):
    peers = samples * heads
    kv_local = kvc_ref.shape[4] // DH
    rollouts, comp_rows = q_ref.shape[1], q_ref.shape[2]
    repeats = q_ref.shape[3] // kvc_ref.shape[4]
    block_rows = kvp_ref.shape[2]
    prefix_rows = block_rows * peers
    all_rows = prefix_rows + comp_rows
    tile_heads = heads_per_tile(prefix_rows)
    tiles = repeats // tile_heads
    tile_rows = tile_heads * comp_rows
    me = lax.axis_index("sample") * heads + lax.axis_index("head")

    def device(block):
        return {"sample": lax.div(block, heads), "head": lax.rem(block, heads)}

    def ahead(j):
        return lax.rem(me + j, peers)

    def behind(j):
        return lax.rem(me + peers - j, peers)

    def rows_of(block):
        return pl.ds(pl.multiple_of(block * block_rows, block_rows), block_rows)

    def lanes_of(block, kv):
        head = lax.rem(block, heads)
        return pl.ds(pl.multiple_of((head * kv_local + kv) * DH, DH), DH)

    def gather_copy(kv, kind, j, to, owner):
        return pltpu.make_async_remote_copy(
            src_ref=kvp_ref.at[kind, 0, :, lanes_of(to, kv)],
            dst_ref=landed.at[kv, kind, rows_of(owner), :],
            send_sem=send_a.at[kv, kind, j],
            recv_sem=recv_a.at[kv, kind, j],
            device_id=device(to),
            device_id_type=MESH,
        )

    def reduce_copy(kv, kind, j, to, owner):
        return pltpu.make_async_remote_copy(
            src_ref=outgoing.at[kv, kind, rows_of(to), :],
            dst_ref=incoming.at[kv, kind, owner],
            send_sem=send_b.at[kv, kind, j],
            recv_sem=recv_b.at[kv, kind, j],
            device_id=device(to),
            device_id_type=MESH,
        )

    def send_prompt(kv, kind):
        for j in range(1, peers):
            gather_copy(kv, kind, j, ahead(j), me).start()

    def prompt_arrived(kv, kind):
        for j in range(1, peers):
            gather_copy(kv, kind, j, ahead(j), behind(j)).wait_recv()

    barrier = pltpu.get_barrier_semaphore()
    for j in range(1, peers):
        pl.semaphore_signal(barrier, inc=1, device_id=device(ahead(j)), device_id_type=MESH)

    row_id = lax.broadcasted_iota(jnp.int32, (comp_rows, comp_rows), 0)
    lane_id = lax.broadcasted_iota(jnp.int32, (comp_rows, comp_rows), 1)
    one_hot = jnp.where(row_id == lane_id, 1.0, 0.0).astype(BF16)
    causal = jnp.where(row_id <= lane_id, 0.0, NEG).astype(BF16)
    prefix_id = lax.broadcasted_iota(jnp.int32, (prefix_rows, comp_rows), 0)
    prefix_bias = jnp.where(prefix_id < plen_ref[0], 0.0, NEG).astype(BF16)
    prefix = pl.ds(0, prefix_rows)
    comp = pl.ds(prefix_rows, comp_rows)
    for r in range(rollouts):
        keys[r, prefix, pl.ds(DH, comp_rows)] = prefix_bias
        keys[r, comp, pl.ds(DH, comp_rows)] = causal
    for kv in range(kv_local):
        landed[kv, :, rows_of(me), :] = kvp_ref[:, 0, :, lanes_of(me, kv)]
    position = lax.rem(
        lax.broadcasted_iota(jnp.int32, (1, tile_rows), 1), jnp.int32(comp_rows)
    )

    pl.semaphore_wait(barrier, peers - 1)
    send_prompt(0, 0)
    send_prompt(0, 1)

    def tile_place(i, kv):
        r = lax.div(i, tiles)
        first = kv * repeats + lax.rem(i, tiles) * tile_heads
        return r, [pl.ds(pl.multiple_of((first + n) * DH, DH), DH) for n in range(tile_heads)]

    def stacked(ref, r, lanes):
        return jnp.concatenate([ref[0, r, :, lane] for lane in lanes], axis=0)

    def each_tile(step):
        lax.fori_loop(0, rollouts * tiles, step, 0, unroll=2)

    def finish(kv, kind, acc, factor):
        mine = pl.ds(kv * DH, DH)
        total = acc[0, prefix, :]
        for r in range(1, rollouts):
            total += acc[r, prefix, :]
        outgoing[kv, kind] = (total * factor).astype(BF16)
        for j in range(1, peers):
            reduce_copy(kv, kind, j, ahead(j), me).start()
        incoming[kv, kind, me] = outgoing[kv, kind, rows_of(me), :]
        for r in range(rollouts):
            gc_ref[kind, 0, r, :, mine] = (acc[r, comp, :] * factor).astype(BF16)

    for kv in range(kv_local):
        mine = pl.ds(kv * DH, DH)
        for r in range(rollouts):
            key_one = kvc_ref[0, 0, r, :, mine]
            value_one = kvc_ref[1, 0, r, :, mine]
            keys[r, comp, pl.ds(0, DH)] = key_one
            values[r, comp, :] = value_one
            keys_t[r, :, comp] = key_one.astype(F32).T.astype(BF16)
            values_t[r, :, comp] = value_one.astype(F32).T.astype(BF16)
        acc_k[...] = jnp.zeros_like(acc_k)
        acc_v[...] = jnp.zeros_like(acc_v)

        prompt_arrived(kv, 0)
        if kv + 1 < kv_local:
            send_prompt(kv + 1, 0)
            send_prompt(kv + 1, 1)
        key_prefix = landed[kv, 0]
        key_prefix_t = key_prefix.astype(F32).T.astype(BF16)
        for r in range(rollouts):
            keys[r, prefix, pl.ds(0, DH)] = key_prefix
            keys_t[r, :, prefix] = key_prefix_t

        def weigh(i, carry, kv=kv):
            r, lanes = tile_place(i, kv)
            query_bias = jnp.concatenate(
                [stacked(q_ref, r, lanes), jnp.concatenate([one_hot] * tile_heads, axis=0)], axis=1
            )
            scores = dot(keys[r], query_bias, ((1,), (1,)))
            row_max = jnp.max(scores, axis=0, keepdims=True)
            exps = jnp.exp2((scores - row_max) * EXP2_SCALE)
            total = jnp.sum(exps, axis=0, keepdims=True)
            inverse = jnp.where(position < clen_ref[0, r], 1.0 / total, 0.0)
            weights32 = exps * inverse
            held[i] = weights32
            acc_v[r] += dot(weights32.astype(BF16), stacked(g_ref, r, lanes), ((1,), (0,)))
            return carry

        each_tile(weigh)
        finish(kv, 1, acc_v, 1.0)

        prompt_arrived(kv, 1)
        value_prefix = landed[kv, 1]
        value_prefix_t = value_prefix.astype(F32).T.astype(BF16)
        for r in range(rollouts):
            values[r, prefix, :] = value_prefix
            values_t[r, :, prefix] = value_prefix_t

        def slope(i, carry, kv=kv):
            r, lanes = tile_place(i, kv)
            grad = stacked(g_ref, r, lanes)
            weights32 = held[i]
            attended_t = dot(values_t[r], weights32.astype(BF16), ((1,), (0,))).astype(BF16).astype(F32)
            delta = jnp.sum(attended_t * grad.astype(F32).T, axis=0, keepdims=True)
            slopes = dot(values[r], grad, ((1,), (1,)))
            ds = (weights32 * (slopes - delta)).astype(BF16)
            held_ds[i] = ds
            attended = attended_t.T.astype(BF16)
            for n in range(tile_heads):
                att_ref[0, r, :, lanes[n]] = attended[n * comp_rows : (n + 1) * comp_rows]
            acc_k[r] += dot(ds, stacked(q_ref, r, lanes), ((1,), (0,)))
            return carry

        each_tile(slope)
        finish(kv, 0, acc_k, SCALE)

        def query_grad(i, carry, kv=kv):
            r, lanes = tile_place(i, kv)
            grad_query = (dot(keys_t[r], held_ds[i], ((1,), (0,))) * SCALE).T.astype(BF16)
            for n in range(tile_heads):
                dq_ref[0, r, :, lanes[n]] = grad_query[n * comp_rows : (n + 1) * comp_rows]
            return carry

        each_tile(query_grad)

    for kv in range(kv_local):
        for kind in (1, 0):
            for j in range(1, peers):
                reduce_copy(kv, kind, j, ahead(j), behind(j)).wait_recv()
            for h in range(heads):
                sum32 = incoming[kv, kind, h].astype(F32)
                for s in range(1, samples):
                    sum32 += incoming[kv, kind, s * heads + h].astype(F32)
                gp_ref[kind, 0, :, pl.ds((h * kv_local + kv) * DH, DH)] = sum32.astype(BF16)
    for kv in range(kv_local):
        for kind in range(2):
            for j in range(1, peers):
                gather_copy(kv, kind, j, ahead(j), me).wait_send()
                reduce_copy(kv, kind, j, ahead(j), me).wait_send()


def write_out(*refs):
    sources, targets, sems = refs[:4], refs[4:8], refs[8]
    copies = [pltpu.make_async_copy(sources[i], targets[i], sems.at[i]) for i in range(4)]
    for copy in copies:
        copy.start()
    for copy in copies:
        copy.wait()


def body(queries, kv_comp, kv_prefix, grad_out, prompt_len, comp_len):
    samples = lax.axis_size("sample")
    heads = lax.axis_size("head")
    peers = samples * heads
    kv_local = kv_comp.shape[4] // DH
    rollouts, comp_rows = queries.shape[1], queries.shape[2]
    block_rows = kv_prefix.shape[2]
    prefix_rows = block_rows * peers
    all_rows = prefix_rows + comp_rows
    tile_heads = heads_per_tile(prefix_rows)
    tile_count = queries.shape[3] // DH // kv_local // tile_heads * rollouts
    vmem = pl.BlockSpec(memory_space=pltpu.VMEM)
    smem = pl.BlockSpec(memory_space=pltpu.SMEM)
    shapes = (queries.shape, queries.shape, kv_comp.shape, kv_prefix.shape)
    results = pl.pallas_call(
        functools.partial(kernel, samples, heads),
        out_shape=tuple(pltpu.VMEM(shape, BF16) for shape in shapes),
        in_specs=[smem, smem, vmem, vmem, vmem, vmem],
        out_specs=(vmem, vmem, vmem, vmem),
        scratch_shapes=[
            pltpu.VMEM((kv_local, 2, prefix_rows, DH), BF16),
            pltpu.VMEM((rollouts, all_rows, DH + comp_rows), BF16),
            pltpu.VMEM((rollouts, all_rows, DH), BF16),
            pltpu.VMEM((rollouts, DH, all_rows), BF16),
            pltpu.VMEM((rollouts, DH, all_rows), BF16),
            pltpu.VMEM((rollouts, all_rows, DH), F32),
            pltpu.VMEM((rollouts, all_rows, DH), F32),
            pltpu.VMEM((tile_count, all_rows, tile_heads * comp_rows), F32),
            pltpu.VMEM((tile_count, all_rows, tile_heads * comp_rows), BF16),
            pltpu.VMEM((kv_local, 2, prefix_rows, DH), BF16),
            pltpu.VMEM((kv_local, 2, peers, block_rows, DH), BF16),
            pltpu.SemaphoreType.DMA((kv_local, 2, peers)),
            pltpu.SemaphoreType.DMA((kv_local, 2, peers)),
            pltpu.SemaphoreType.DMA((kv_local, 2, peers)),
            pltpu.SemaphoreType.DMA((kv_local, 2, peers)),
        ],
        compiler_params=pltpu.CompilerParams(
            collective_id=0, has_side_effects=True, vmem_limit_bytes=60 * 1024 * 1024
        ),
    )(prompt_len, comp_len, queries, grad_out, kv_comp, kv_prefix)
    return pl.pallas_call(
        write_out,
        out_shape=tuple(jax.ShapeDtypeStruct(shape, BF16) for shape in shapes),
        in_specs=[pl.BlockSpec(memory_space=pl.ANY)] * 4,
        out_specs=(pl.BlockSpec(memory_space=pl.ANY),) * 4,
        scratch_shapes=[pltpu.SemaphoreType.DMA((4,))],
        compiler_params=pltpu.CompilerParams(vmem_limit_bytes=1024 * 1024),
    )(*results)


def solution(mesh):
    return jax.shard_map(
        body,
        mesh=mesh,
        in_specs=(
            P("group", "sample", None, "head"),
            P(None, "group", "sample", None, "head"),
            P(None, "group", ("sample", "head"), None),
            P("group", "sample", None, "head"),
            P("group"),
            P("group", "sample"),
        ),
        out_specs=(
            P("group", "sample", None, "head"),
            P("group", "sample", None, "head"),
            P(None, "group", "sample", None, "head"),
            P(None, "group", ("sample", "head"), None),
        ),
        check_vma=False,
    )
```

```python
import functools

import jax
import jax.numpy as jnp
from jax import lax
from jax.experimental import pallas as pl
from jax.experimental.pallas import tpu as pltpu
from jax.sharding import PartitionSpec as P

DH = 128
NEG = -1e30
MESH = pl.DeviceIdType.MESH
SCALE = 1.0 / DH**0.5
EXP2_SCALE = SCALE * 1.4426950408889634
F32 = jnp.float32
BF16 = jnp.bfloat16


def heads_per_tile(prefix_rows):
    return 8 if prefix_rows <= 1024 else 2


def dot(a, b, dims):
    return lax.dot_general(a, b, (dims, ((), ())), preferred_element_type=F32)


def kernel(
    samples,
    heads,
    plen_ref,
    clen_ref,
    q_any,
    g_any,
    kvc_ref,
    kvp_ref,
    att_ref,
    dq_ref,
    gc_ref,
    gp_ref,
    landed,
    keys,
    values,
    keys_t,
    values_t,
    acc_k,
    acc_v,
    held,
    held_ds,
    outgoing,
    own,
    incoming,
    summed,
    final,
    last,
    q_ref,
    g_ref,
    load_sem,
    send_a,
    recv_a,
    send_b,
    recv_b,
    send_c,
    recv_c,
    send_d,
    recv_d,
):
    peers = samples * heads
    kv_local = kvc_ref.shape[4] // DH
    rollouts, comp_rows = q_ref.shape[1], q_ref.shape[2]
    repeats = q_ref.shape[3] // kvc_ref.shape[4]
    block_rows = kvp_ref.shape[2]
    prefix_rows = block_rows * peers
    all_rows = prefix_rows + comp_rows
    tile_heads = heads_per_tile(prefix_rows)
    tiles = repeats // tile_heads
    tile_rows = tile_heads * comp_rows
    span = block_rows * heads
    my_sample, my_head = lax.axis_index("sample"), lax.axis_index("head")
    me = my_sample * heads + my_head

    def other_head(j):
        return lax.rem(my_head + j + heads, heads)

    def other_sample(j):
        return lax.rem(my_sample + j + samples, samples)

    def rows_of(block):
        return pl.ds(pl.multiple_of(block * block_rows, block_rows), block_rows)

    def span_of(sample):
        return pl.ds(pl.multiple_of(sample * span, span), span)

    def lanes_of(head, kv):
        return pl.ds(pl.multiple_of((head * kv_local + kv) * DH, DH), DH)

    def device(block):
        return {"sample": lax.div(block, heads), "head": lax.rem(block, heads)}

    def ahead(j):
        return lax.rem(me + j, peers)

    def behind(j):
        return lax.rem(me + peers - j, peers)

    def gather_copy(kv, kind, j, owner):
        to = ahead(j)
        return pltpu.make_async_remote_copy(
            src_ref=kvp_ref.at[kind, 0, :, lanes_of(lax.rem(to, heads), kv)],
            dst_ref=landed.at[kv, kind, rows_of(owner), :],
            send_sem=send_a.at[kv, kind, j],
            recv_sem=recv_a.at[kv, kind, j],
            device_id=device(to),
            device_id_type=MESH,
        )

    def reduce_copy(j, owner):
        to = ahead(j)
        return pltpu.make_async_remote_copy(
            src_ref=outgoing.at[kv_local - 1, 0, rows_of(to), :],
            dst_ref=last.at[owner],
            send_sem=send_b.at[j],
            recv_sem=recv_b.at[j],
            device_id=device(to),
            device_id_type=MESH,
        )

    def reduce_sample(kv, kind, j):
        return pltpu.make_async_remote_copy(
            src_ref=outgoing.at[kv, kind, span_of(other_sample(j)), :],
            dst_ref=incoming.at[kv, kind, j],
            send_sem=send_c.at[kv, kind, j],
            recv_sem=recv_c.at[kv, kind, j],
            device_id={"sample": other_sample(j)},
            device_id_type=MESH,
        )

    def reduce_head(kv, kind, j):
        return pltpu.make_async_remote_copy(
            src_ref=summed.at[kv, kind, pl.ds(pl.multiple_of(other_head(j) * block_rows, block_rows), block_rows), :],
            dst_ref=final.at[kv, kind, my_head],
            send_sem=send_d.at[kv, kind, j],
            recv_sem=recv_d.at[kv, kind, j],
            device_id={"head": other_head(j)},
            device_id_type=MESH,
        )

    def landing_final(kv, kind, j):
        place = final.at[kv, kind, other_head(-j)]
        return pltpu.make_async_remote_copy(
            src_ref=place,
            dst_ref=place,
            send_sem=send_d.at[kv, kind, j],
            recv_sem=recv_d.at[kv, kind, j],
            device_id={"head": other_head(j)},
            device_id_type=MESH,
        )

    def send_prompt(kv, kind):
        for j in range(1, peers):
            gather_copy(kv, kind, j, me).start()

    def prompt_arrived(kv, kind):
        for j in range(1, peers):
            gather_copy(kv, kind, j, behind(j)).wait_recv()

    def pass_gradient(kv, kind):
        sum32 = own[kv, kind]
        for j in range(1, samples):
            reduce_sample(kv, kind, j).wait_recv()
        for j in range(1, samples):
            sum32 += incoming[kv, kind, j].astype(F32)
        summed[kv, kind] = sum32.astype(BF16)
        for j in range(1, heads):
            reduce_head(kv, kind, j).start()
        mine = pl.ds(pl.multiple_of(my_head * block_rows, block_rows), block_rows)
        final[kv, kind, my_head] = summed[kv, kind, mine, :]

    loads = [
        pltpu.make_async_copy(q_any, q_ref, load_sem.at[0]),
        pltpu.make_async_copy(g_any, g_ref, load_sem.at[1]),
    ]
    for load in loads:
        load.start()
    barrier = pltpu.get_barrier_semaphore()
    for j in range(1, peers):
        pl.semaphore_signal(barrier, inc=1, device_id=device(ahead(j)), device_id_type=MESH)

    row_id = lax.broadcasted_iota(jnp.int32, (comp_rows, comp_rows), 0)
    lane_id = lax.broadcasted_iota(jnp.int32, (comp_rows, comp_rows), 1)
    one_hot = jnp.where(row_id == lane_id, 1.0, 0.0).astype(BF16)
    causal = jnp.where(row_id <= lane_id, 0.0, NEG).astype(BF16)
    prefix_id = lax.broadcasted_iota(jnp.int32, (prefix_rows, comp_rows), 0)
    prefix_bias = jnp.where(prefix_id < plen_ref[0], 0.0, NEG).astype(BF16)
    prefix = pl.ds(0, prefix_rows)
    comp = pl.ds(prefix_rows, comp_rows)
    for r in range(rollouts):
        keys[r, prefix, pl.ds(DH, comp_rows)] = prefix_bias
        keys[r, comp, pl.ds(DH, comp_rows)] = causal
    for kv in range(kv_local):
        landed[kv, :, rows_of(me), :] = kvp_ref[:, 0, :, lanes_of(my_head, kv)]
    position = lax.rem(
        lax.broadcasted_iota(jnp.int32, (1, tile_rows), 1), jnp.int32(comp_rows)
    )

    pl.semaphore_wait(barrier, peers - 1)
    send_prompt(0, 0)
    send_prompt(0, 1)
    for load in loads:
        load.wait()

    def tile_place(i, kv):
        r = lax.div(i, tiles)
        first = kv * repeats + lax.rem(i, tiles) * tile_heads
        return r, [pl.ds(pl.multiple_of((first + n) * DH, DH), DH) for n in range(tile_heads)]

    def stacked(ref, r, lanes):
        return jnp.concatenate([ref[0, r, :, lane] for lane in lanes], axis=0)

    def each_tile(step):
        lax.fori_loop(0, rollouts * tiles, step, 0, unroll=2)

    def finish(kv, kind, acc, factor):
        mine = pl.ds(kv * DH, DH)
        total = acc[0, prefix, :]
        for r in range(1, rollouts):
            total += acc[r, prefix, :]
        outgoing[kv, kind] = (total * factor).astype(BF16)
        if (kv, kind) == (kv_local - 1, 0):
            for j in range(1, peers):
                reduce_copy(j, me).start()
            last[me] = outgoing[kv, kind, rows_of(me), :]
        else:
            for j in range(1, samples):
                reduce_sample(kv, kind, j).start()
            rows = span_of(my_sample)
            own32 = acc[0, rows, :]
            for r in range(1, rollouts):
                own32 += acc[r, rows, :]
            own[kv, kind] = own32 * factor
        for r in range(rollouts):
            gc_ref[kind, 0, r, :, mine] = (acc[r, comp, :] * factor).astype(BF16)

    for kv in range(kv_local):
        mine = pl.ds(kv * DH, DH)
        for r in range(rollouts):
            key_one = kvc_ref[0, 0, r, :, mine]
            value_one = kvc_ref[1, 0, r, :, mine]
            keys[r, comp, pl.ds(0, DH)] = key_one
            values[r, comp, :] = value_one
            keys_t[r, :, comp] = key_one.astype(F32).T.astype(BF16)
            values_t[r, :, comp] = value_one.astype(F32).T.astype(BF16)
        acc_k[...] = jnp.zeros_like(acc_k)
        acc_v[...] = jnp.zeros_like(acc_v)

        prompt_arrived(kv, 0)
        if kv + 1 < kv_local:
            send_prompt(kv + 1, 0)
            send_prompt(kv + 1, 1)
        key_prefix = landed[kv, 0]
        key_prefix_t = key_prefix.astype(F32).T.astype(BF16)
        for r in range(rollouts):
            keys[r, prefix, pl.ds(0, DH)] = key_prefix
            keys_t[r, :, prefix] = key_prefix_t

        def weigh(i, carry, kv=kv):
            r, lanes = tile_place(i, kv)
            query_bias = jnp.concatenate(
                [stacked(q_ref, r, lanes), jnp.concatenate([one_hot] * tile_heads, axis=0)], axis=1
            )
            scores = dot(keys[r], query_bias, ((1,), (1,)))
            row_max = jnp.max(scores, axis=0, keepdims=True)
            exps = jnp.exp2((scores - row_max) * EXP2_SCALE)
            total = jnp.sum(exps, axis=0, keepdims=True)
            inverse = jnp.where(position < clen_ref[0, r], 1.0 / total, 0.0)
            weights32 = exps * inverse
            held[i] = weights32
            acc_v[r] += dot(weights32.astype(BF16), stacked(g_ref, r, lanes), ((1,), (0,)))
            return carry

        each_tile(weigh)
        finish(kv, 1, acc_v, 1.0)
        if kv > 0:
            pass_gradient(kv - 1, 0)

        prompt_arrived(kv, 1)
        value_prefix = landed[kv, 1]
        value_prefix_t = value_prefix.astype(F32).T.astype(BF16)
        for r in range(rollouts):
            values[r, prefix, :] = value_prefix
            values_t[r, :, prefix] = value_prefix_t

        def slope(i, carry, kv=kv):
            r, lanes = tile_place(i, kv)
            grad = stacked(g_ref, r, lanes)
            weights32 = held[i]
            attended_t = dot(values_t[r], weights32.astype(BF16), ((1,), (0,))).astype(BF16).astype(F32)
            delta = jnp.sum(attended_t * grad.astype(F32).T, axis=0, keepdims=True)
            slopes = dot(values[r], grad, ((1,), (1,)))
            ds = (weights32 * (slopes - delta)).astype(BF16)
            held_ds[i] = ds
            attended = attended_t.T.astype(BF16)
            for n in range(tile_heads):
                att_ref[0, r, :, lanes[n]] = attended[n * comp_rows : (n + 1) * comp_rows]
            acc_k[r] += dot(ds, stacked(q_ref, r, lanes), ((1,), (0,)))
            return carry

        each_tile(slope)
        finish(kv, 0, acc_k, SCALE)
        pass_gradient(kv, 1)

        def query_grad(i, carry, kv=kv):
            r, lanes = tile_place(i, kv)
            grad_query = (dot(keys_t[r], held_ds[i], ((1,), (0,))) * SCALE).T.astype(BF16)
            for n in range(tile_heads):
                dq_ref[0, r, :, lanes[n]] = grad_query[n * comp_rows : (n + 1) * comp_rows]
            return carry

        each_tile(query_grad)

    two_step = [(kv, kind) for kv in range(kv_local) for kind in (1, 0)][:-1]
    for kv, kind in two_step:
        for j in range(1, heads):
            landing_final(kv, kind, j).wait_recv()
        for h in range(heads):
            gp_ref[kind, 0, :, pl.ds((h * kv_local + kv) * DH, DH)] = final[kv, kind, h]
    for j in range(1, peers):
        reduce_copy(j, behind(j)).wait_recv()
    for h in range(heads):
        sum32 = last[h].astype(F32)
        for s in range(1, samples):
            sum32 += last[s * heads + h].astype(F32)
        gp_ref[0, 0, :, pl.ds((h * kv_local + kv_local - 1) * DH, DH)] = sum32.astype(BF16)
    for kv in range(kv_local):
        for kind in range(2):
            for j in range(1, peers):
                gather_copy(kv, kind, j, me).wait_send()
    for kv, kind in two_step:
        for j in range(1, heads):
            reduce_head(kv, kind, j).wait_send()
        for j in range(1, samples):
            reduce_sample(kv, kind, j).wait_send()
    for j in range(1, peers):
        reduce_copy(j, me).wait_send()


def write_out(*refs):
    sources, targets, sems = refs[:4], refs[4:8], refs[8]
    copies = [pltpu.make_async_copy(sources[i], targets[i], sems.at[i]) for i in range(4)]
    for copy in copies:
        copy.start()
    for copy in copies:
        copy.wait()


def body(queries, kv_comp, kv_prefix, grad_out, prompt_len, comp_len):
    samples = lax.axis_size("sample")
    heads = lax.axis_size("head")
    peers = samples * heads
    kv_local = kv_comp.shape[4] // DH
    rollouts, comp_rows = queries.shape[1], queries.shape[2]
    block_rows = kv_prefix.shape[2]
    prefix_rows = block_rows * peers
    all_rows = prefix_rows + comp_rows
    tile_heads = heads_per_tile(prefix_rows)
    tile_count = queries.shape[3] // DH // kv_local // tile_heads * rollouts
    vmem = pl.BlockSpec(memory_space=pltpu.VMEM)
    hbm = pl.BlockSpec(memory_space=pl.ANY)
    smem = pl.BlockSpec(memory_space=pltpu.SMEM)
    shapes = (queries.shape, queries.shape, kv_comp.shape, kv_prefix.shape)
    results = pl.pallas_call(
        functools.partial(kernel, samples, heads),
        out_shape=tuple(pltpu.VMEM(shape, BF16) for shape in shapes),
        in_specs=[smem, smem, hbm, hbm, vmem, vmem],
        out_specs=(vmem, vmem, vmem, vmem),
        scratch_shapes=[
            pltpu.VMEM((kv_local, 2, prefix_rows, DH), BF16),
            pltpu.VMEM((rollouts, all_rows, DH + comp_rows), BF16),
            pltpu.VMEM((rollouts, all_rows, DH), BF16),
            pltpu.VMEM((rollouts, DH, all_rows), BF16),
            pltpu.VMEM((rollouts, DH, all_rows), BF16),
            pltpu.VMEM((rollouts, all_rows, DH), F32),
            pltpu.VMEM((rollouts, all_rows, DH), F32),
            pltpu.VMEM((tile_count, all_rows, tile_heads * comp_rows), F32),
            pltpu.VMEM((tile_count, all_rows, tile_heads * comp_rows), BF16),
            pltpu.VMEM((kv_local, 2, prefix_rows, DH), BF16),
            pltpu.VMEM((kv_local, 2, block_rows * heads, DH), F32),
            pltpu.VMEM((kv_local, 2, samples, block_rows * heads, DH), BF16),
            pltpu.VMEM((kv_local, 2, block_rows * heads, DH), BF16),
            pltpu.VMEM((kv_local, 2, heads, block_rows, DH), BF16),
            pltpu.VMEM((peers, block_rows, DH), BF16),
            pltpu.VMEM(queries.shape, BF16),
            pltpu.VMEM(queries.shape, BF16),
            pltpu.SemaphoreType.DMA((2,)),
            pltpu.SemaphoreType.DMA((kv_local, 2, peers)),
            pltpu.SemaphoreType.DMA((kv_local, 2, peers)),
            pltpu.SemaphoreType.DMA((peers,)),
            pltpu.SemaphoreType.DMA((peers,)),
            pltpu.SemaphoreType.DMA((kv_local, 2, samples)),
            pltpu.SemaphoreType.DMA((kv_local, 2, samples)),
            pltpu.SemaphoreType.DMA((kv_local, 2, heads)),
            pltpu.SemaphoreType.DMA((kv_local, 2, heads)),
        ],
        compiler_params=pltpu.CompilerParams(
            collective_id=0, has_side_effects=True, vmem_limit_bytes=58 * 1024 * 1024
        ),
    )(prompt_len, comp_len, queries, grad_out, kv_comp, kv_prefix)
    return pl.pallas_call(
        write_out,
        out_shape=tuple(jax.ShapeDtypeStruct(shape, BF16) for shape in shapes),
        in_specs=[hbm] * 4,
        out_specs=(hbm,) * 4,
        scratch_shapes=[pltpu.SemaphoreType.DMA((4,))],
        compiler_params=pltpu.CompilerParams(vmem_limit_bytes=1024 * 1024),
    )(*results)


def solution(mesh):
    return jax.shard_map(
        body,
        mesh=mesh,
        in_specs=(
            P("group", "sample", None, "head"),
            P(None, "group", "sample", None, "head"),
            P(None, "group", ("sample", "head"), None),
            P("group", "sample", None, "head"),
            P("group"),
            P("group", "sample"),
        ),
        out_specs=(
            P("group", "sample", None, "head"),
            P("group", "sample", None, "head"),
            P(None, "group", "sample", None, "head"),
            P(None, "group", ("sample", "head"), None),
        ),
        check_vma=False,
    )
```
